256 devices in a mesh: seq: 64 (over x_lo, y, z), chrom: 4 (over x_hi, core).
Axes of the slice: x: 4 (x_hi: 2, x_lo: 2; x = x_hi * 2 + x_lo), y: 4, z: 8, core: 2. Of those that a mesh axis runs over, the one named last changes fastest.
Arguments:
- features: bfloat16 [4, 40960, 768], P('chrom', 'seq'), may hold values from -6 to 6
- first_dilated_taps: bfloat16 [3, 768, 384], replicated, may hold values from -0.125 to 0.125
- first_norm_scale: float32 [384], replicated, may hold values from 0.5 to 2
- first_norm_offset: float32 [384], replicated, may hold values from -3 to 3
- first_pointwise_weight: bfloat16 [384, 768], replicated, may hold values from -0.3125 to 0.3125
- second_dilated_taps: bfloat16 [3, 768, 384], replicated, may hold values from -0.125 to 0.125
- second_norm_scale: float32 [384], replicated, may hold values from 0.5 to 2
- second_norm_offset: float32 [384], replicated, may hold values from -3 to 3
- second_pointwise_weight: bfloat16 [384, 768], replicated, may hold values from -0.3125 to 0.3125
- cotangent: bfloat16 [4, 40960, 768], P('chrom', 'seq'), may hold values from -16 to 16
Outputs:
- grad_input: bfloat16 [4, 40960, 768], P('chrom', 'seq')
- grad_conv_a: float32 [3, 768, 384], P(None, 'seq')
- grad_point_a: float32 [384, 768], P(None, 'seq')
- grad_scale_a: float32 [384], replicated
- grad_shift_a: float32 [384], replicated
- grad_conv_b: float32 [3, 768, 384], P(None, 'seq')
- grad_point_b: float32 [384, 768], P(None, 'seq')
- grad_scale_b: float32 [384], replicated
- grad_shift_b: float32 [384], replicated
The draws below stay inside these ranges and needn't reach their ends.
All inputs are finite; a program needn't handle non-finite values.
Results may differ from the reference program's by a relative error of at most 0.018.
Values may be sent and summed in bfloat16 or wider, within the bound.
A program may use at most 128 MiB of HBM per device.

```python
import math
import jax
import jax.numpy as jnp
from jax import lax

C = 768
F = 384
DILATION_FIRST = 4096
DILATION_SECOND = 2048
BINS = 40960
CHROMS = 4


def spiked(array, rng, source, target, blocks, factor):
    owner, partner = [(jnp.arange(array.shape[dim]) // (array.shape[dim] // blocks)).reshape([-1 if axis == dim else 1 for axis in range(array.ndim)]) for dim in (source, target)]
    chosen = jax.random.permutation(rng, blocks)[partner]
    strong = (owner == chosen) | (owner == (partner + blocks // 2) % blocks)
    return jnp.where(strong, factor * array, array)


def levels(own_key, shape, split, low, top_value):
    level, own = 1.0, jax.random.fold_in(own_key, 6)
    for axis_at, shards_of in split:
        heights = jnp.exp(jax.random.uniform(jax.random.fold_in(own, axis_at), (shards_of,), jnp.float32, low / len(split), top_value / len(split)))
        level = level * jnp.repeat(heights, shape[axis_at] // shards_of).reshape([-1 if axis == axis_at else 1 for axis in range(len(shape))])
    return level


def centred(key, dims, width, reach, split=(), held_as=jnp.bfloat16):
    drawn = jax.random.normal(key, dims, jnp.float32) * width
    if len(split) > 0:
        drawn = levels(key, dims, split, -0.22, 0.18) * drawn
    return jnp.clip(drawn, min=-reach, max=reach).astype(held_as)


def bell_draw_with(own_key, extent, spread, most, cuts, heavy, held_as=jnp.bfloat16):
    result = spread * jax.random.normal(own_key, extent, jnp.float32)
    if cuts:
        result = result * levels(own_key, extent, cuts, -0.22, 0.18)
    return jnp.clip(spiked(result, jax.random.fold_in(own_key, 3), *heavy), -most, most).astype(held_as)


def setup_inputs(seed: int = 0) -> dict:
    seeds = jax.random.split(jax.random.key(seed), 11)
    features = centred(seeds[0], (CHROMS, BINS, C), 1.0, 6.0, ((0, 4), (1, 64)))
    first_dilated_taps = centred(seeds[1], (3, C, F), (3 * C) ** -0.5, 0.125)
    first_norm_scale = jnp.clip(jnp.exp(jax.random.uniform(seeds[2], (F,), jnp.float32, math.log(0.5), math.log(2.0))), 0.5, 2.0)
    first_norm_offset = centred(seeds[3], (F,), 0.5, 3.0, (), jnp.float32)
    first_pointwise_weight = centred(seeds[4], (F, C), F ** -0.5, 0.3125)
    second_dilated_taps = centred(seeds[5], (3, C, F), (3 * C) ** -0.5, 0.125)
    second_norm_scale = jnp.clip(jnp.exp(jax.random.uniform(seeds[6], (F,), jnp.float32, math.log(0.5), math.log(2.0))), 0.5, 2.0)
    second_norm_offset = centred(seeds[7], (F,), 0.5, 3.0, (), jnp.float32)
    second_pointwise_weight = centred(seeds[8], (F, C), F ** -0.5, 0.3125)
    cotangent = bell_draw_with(seeds[9], (CHROMS, BINS, C), 1.0, 16.0, ((0, 4), (1, 64)), (1, 2, 64, 4.0))
    return {"features": features, "first_dilated_taps": first_dilated_taps, "first_norm_scale": first_norm_scale, "first_norm_offset": first_norm_offset, "first_pointwise_weight": first_pointwise_weight, "second_dilated_taps": second_dilated_taps, "second_norm_scale": second_norm_scale, "second_norm_offset": second_norm_offset, "second_pointwise_weight": second_pointwise_weight, "cotangent": cotangent}


def smooth_value(normed):
    return normed * jax.nn.sigmoid(1.702 * normed)

def smooth_slope(normed):
    sigmoid_part = jax.nn.sigmoid(1.702 * normed)
    return sigmoid_part * (1.0 + 1.702 * normed * (1.0 - sigmoid_part))

def displaced(field, offset):
    rows_all = field.shape[0]
    zero_rows = jnp.zeros((abs(offset), field.shape[1]), field.dtype)
    if offset > 0:
        return jnp.concatenate([field[offset:], zero_rows], 0)
    return jnp.concatenate([zero_rows, field[:rows_all + offset]], 0)

def bottleneck_block_ahead(inputs, conv_weight, bn_scale, bn_shift, dilation):
    before = displaced(inputs, -dilation)
    after = displaced(inputs, dilation)
    pre_act = jnp.dot(before, conv_weight[0], preferred_element_type=jnp.float32)
    pre_act = pre_act + jnp.dot(inputs, conv_weight[1], preferred_element_type=jnp.float32)
    pre_act = pre_act + jnp.dot(after, conv_weight[2], preferred_element_type=jnp.float32)
    normed = bn_scale * pre_act + bn_shift
    activated = smooth_value(normed).astype(jnp.bfloat16)
    return (before, after, pre_act, normed, activated)

def bottleneck_block_reverse(inputs, saved, conv_weight, bn_scale, point_weight, upstream, dilation):
    before, after, pre_act, normed, activated = saved
    grad_act = jnp.dot(upstream, point_weight.T, preferred_element_type=jnp.float32)
    grad_norm = grad_act * smooth_slope(normed)
    grad_pre = (grad_norm * bn_scale).astype(jnp.bfloat16)
    grad_point = jnp.dot(activated.T, upstream, preferred_element_type=jnp.float32)
    grad_scale = lax.optimization_barrier(jnp.sum(grad_norm * pre_act, 0))
    grad_shift = lax.optimization_barrier(jnp.sum(grad_norm, 0))
    grad_conv = jnp.stack([jnp.dot(before.T, grad_pre, preferred_element_type=jnp.float32), jnp.dot(inputs.T, grad_pre, preferred_element_type=jnp.float32), jnp.dot(after.T, grad_pre, preferred_element_type=jnp.float32)])
    grad_in = upstream.astype(jnp.float32) + jnp.dot(grad_pre, conv_weight[1].T, preferred_element_type=jnp.float32)
    grad_in = grad_in + displaced(jnp.dot(grad_pre, conv_weight[0].T, preferred_element_type=jnp.float32), dilation)
    grad_in = grad_in + displaced(jnp.dot(grad_pre, conv_weight[2].T, preferred_element_type=jnp.float32), -dilation)
    return (grad_in.astype(jnp.bfloat16), (grad_conv, grad_point, grad_scale, grad_shift))

def reference(features, first_dilated_taps, first_norm_scale, first_norm_offset, first_pointwise_weight, second_dilated_taps, second_norm_scale, second_norm_offset, second_pointwise_weight, cotangent):
    inputs_out = []
    totals_a = None
    totals_b = None
    for chromosome_index in range(CHROMS):
        first_block_output = features[chromosome_index]
        first_block_stash = bottleneck_block_ahead(first_block_output, first_dilated_taps, first_norm_scale, first_norm_offset, DILATION_FIRST)
        second_block_output = (first_block_output.astype(jnp.float32) + jnp.dot(first_block_stash[4], first_pointwise_weight, preferred_element_type=jnp.float32)).astype(jnp.bfloat16)
        second_block_stash = bottleneck_block_ahead(second_block_output, second_dilated_taps, second_norm_scale, second_norm_offset, DILATION_SECOND)
        second_block_gradient, second_block_partials = bottleneck_block_reverse(second_block_output, second_block_stash, second_dilated_taps, second_norm_scale, second_pointwise_weight, cotangent[chromosome_index], DILATION_SECOND)
        first_block_gradient, first_block_partials = bottleneck_block_reverse(first_block_output, first_block_stash, first_dilated_taps, first_norm_scale, first_pointwise_weight, second_block_gradient, DILATION_FIRST)
        inputs_out.append(first_block_gradient)
        if totals_a is None:
            totals_a, totals_b = (first_block_partials, second_block_partials)
        else:
            totals_a = jax.tree.map(jnp.add, totals_a, first_block_partials)
            totals_b = jax.tree.map(jnp.add, totals_b, second_block_partials)
    factor = 1.0 / math.sqrt(CHROMS * BINS)
    totals_a = [item * factor for item in totals_a]
    totals_b = [item * factor for item in totals_b]
    return (jnp.stack(inputs_out), totals_a[0], totals_a[1], totals_a[2], totals_a[3], totals_b[0], totals_b[1], totals_b[2], totals_b[3])
```

```python
import math

import jax
import jax.numpy as jnp
from jax import lax
from jax.experimental import pallas as pl
from jax.experimental.pallas import tpu as pltpu
from jax.sharding import PartitionSpec as P

MESH = pl.DeviceIdType.MESH
F32 = jnp.float32
BF16 = jnp.bfloat16
C = 768
F = 384
NB = 20
RB = 32
HALF = 10
NC = 64
ACT = 24


def device_of(c):
    return c


def class_of(d):
    return d


def dot(a, b):
    return jnp.dot(a, b, preferred_element_type=F32)


def dot_t(a, b):
    return lax.dot_general(a, b, (((1,), (1,)), ((), ())), preferred_element_type=F32)


def rows(ref, start, count):
    value = ref[pl.ds(start, count)]
    return value.reshape(count * RB, value.shape[-1])


def loop(n, step):
    def run(i, carry):
        step(i)
        return carry

    lax.fori_loop(0, n, run, 0)


def kernel(
    feat, wa_h, sa_h, ba_h, pa_h, wb_h, sb_h, bb_h, pb_h, cot,
    out, gca, gpa, gna, gcb, gpb, gnb,
    u, c, s, gs, gi, sl_a, sl_b, pr_a, pr_b, rh_a, rh_b, lt_a, lt_b,
    wa, wb, pa, pb, nv,
    own_a, own_b, cs_a, cs_b, cr_a, cr_b,
    a1s, a1r, a2s, a2r, b1s, b1r, b2s, b2r, red_a, red_b, zs, zr, fg,
    nbs, nbc, nbx, nby, nbz,
    sem_w, su, ru, sc, rc, so, ro,
    sem_cs, sem_cr, sa1, ra1, sa2, ra2, sb1, rb1, sb2, rb2, sz, rz, sf, rf,
    snc, rnc, snx, rnx, sny, rny, snz, rnz,
):
    d = lax.axis_index("seq")
    k = lax.axis_index("chrom")
    xlo, y, z = d // 32, (d // 8) % 4, d % 8
    xhi, core = k // 2, k % 2
    x = 2 * xhi + xlo
    cls = class_of(d)
    first = NB * d

    def home_of(j):
        return (cls + NC * j) // NB

    def to_x(t):
        return {"seq": (t % 2) * 32 + d % 32, "chrom": 2 * (t // 2) + core}

    def to_y(t):
        return {"seq": xlo * 32 + t * 8 + z, "chrom": k}

    def to_z(t):
        return {"seq": xlo * 32 + y * 8 + t, "chrom": k}

    def to_k(t):
        return {"seq": d, "chrom": t}

    partner = to_k(2 * xhi + 1 - core)

    barrier = pltpu.get_barrier_semaphore()

    def greet(where):
        pl.semaphore_signal(barrier, inc=1, device_id=where, device_id_type=MESH)

    def greet_block(i, count):
        home = home_of(i)
        target = device_of((first + i) % NC)

        @pl.when(home != d)
        def _():
            greet({"seq": home, "chrom": k})

        @pl.when(target != d)
        def _():
            greet({"seq": target, "chrom": k})

        return count + jnp.where(home != d, 1, 0) + jnp.where(target != d, 1, 0)

    greeted = lax.fori_loop(0, NB, greet_block, 0)
    for r in range(1, 4):
        greet(to_x((x + r) % 4))
        greet(to_y((y + r) % 4))
        greet(to_k((k + r) % 4))
    for r in range(1, 8):
        greet(to_z((z + r) % 8))
    pl.semaphore_wait(barrier, greeted + 16)

    def send_in(src, dst, pad, send, recv):
        def step(i):
            q = first + i
            target = device_of(q % NC)
            slot = q // NC

            @pl.when(target != d)
            def _():
                pltpu.make_async_remote_copy(
                    src.at[i], dst.at[slot + pad], send.at[i], recv.at[slot],
                    device_id={"seq": target, "chrom": k}, device_id_type=MESH,
                ).start()

            @pl.when(target == d)
            def _():
                pltpu.make_async_copy(src.at[i], dst.at[slot + pad], recv.at[slot]).start()

        loop(NB, step)

    send_in(feat, u, 2, su, ru)
    loads = [
        (wa_h, wa), (wb_h, wb), (pa_h, pa), (pb_h, pb),
        (sa_h, nv.at[pl.ds(0, 1)]), (ba_h, nv.at[pl.ds(1, 1)]),
        (sb_h, nv.at[pl.ds(2, 1)]), (bb_h, nv.at[pl.ds(3, 1)]),
    ]
    loads = [pltpu.make_async_copy(a, b, sem_w.at[n]) for n, (a, b) in enumerate(loads)]
    for load in loads:
        load.start()
    send_in(cot, c, 0, sc, rc)

    for ref, count in ((u, 2), (s, 1), (rh_a, 2), (rh_b, 1)):
        zero = jnp.zeros((count,) + ref.shape[1:], BF16)
        ref[pl.ds(0, count)] = zero
        ref[pl.ds(NB + count, count)] = zero
    for load in loads:
        load.wait()

    loop(NB, lambda j: pltpu.make_async_copy(feat.at[0], u.at[j + 2], ru.at[j]).wait())

    def turn(src, pad, dst, which):
        for n in range(5):
            tile = rows(src, 4 * n + pad, 4)
            dst[which, :, n * 128 : (n + 1) * 128] = tile.T

    def ahead(src, shift, w, scale, offset, pre_ref, slope_ref, right):
        def step(n):
            at = n * HALF
            pre = dot(rows(src, at, HALF), w[0])
            pre = pre + dot(rows(src, at + shift, HALF), w[1])
            pre = pre + dot(rows(src, at + 2 * shift, HALF), w[2])
            normed = scale * pre + offset
            q = jax.nn.sigmoid(1.702 * normed)
            act = (normed * q).astype(BF16)
            pre_ref[n] = pre
            slope_ref[n] = q * (1.0 + 1.702 * normed * (1.0 - q))
            right[pl.ds(ACT + at, HALF)] = act.reshape(HALF, RB, F)
            if shift == 2:
                second = rows(src, at + 2, HALF).astype(F32) + dot(act, pa[...])
                s[pl.ds(at + 1, HALF)] = second.astype(BF16).reshape(HALF, RB, C)

        loop(2, step)

    ahead(u, 2, wa, nv[0:1], nv[1:2], pr_a, sl_a, rh_a)
    ahead(s, 1, wb, nv[2:3], nv[3:4], pr_b, sl_b, rh_b)
    turn(u, 2, lt_a, 0)
    turn(s, 1, lt_b, 0)
    nbs[...] = jnp.zeros_like(nbs)

    loop(NB, lambda j: pltpu.make_async_copy(cot.at[0], c.at[j], rc.at[j]).wait())

    def back_act(grad, p, scale, shift, pre_ref, slope_ref, right, row):
        def step(n):
            at = n * HALF
            grad_norm = dot_t(rows(grad, at, HALF), p[...]) * slope_ref[n]
            right[pl.ds(at + shift, HALF)] = (
                (grad_norm * scale).astype(BF16).reshape(HALF, RB, F)
            )
            nbs[row : row + 1] += jnp.sum(grad_norm * pre_ref[n], 0, keepdims=True)
            nbs[row + 1 : row + 2] += jnp.sum(grad_norm, 0, keepdims=True)

        loop(2, step)

    def back_in(grad, w, shift, right, dst):
        def step(n):
            at = n * HALF
            total = rows(grad, at, HALF).astype(F32)
            total = total + dot_t(rows(right, at + shift, HALF), w[1])
            total = total + dot_t(rows(right, at + 2 * shift, HALF), w[0])
            total = total + dot_t(rows(right, at, HALF), w[2])
            dst[pl.ds(at, HALF)] = total.astype(BF16).reshape(HALF, RB, C)

        loop(2, step)

    def part(left, right, shift, t, half):
        start = jnp.where(t == 3, ACT, 2 * shift - shift * t)
        return dot(left[t // 3, pl.ds(half * 384, 384), :], rows(right, start, NB))

    def core_copy(n, p):
        cs, cr = ((cs_a, cr_a), (cs_b, cr_b))[n]
        return pltpu.make_async_remote_copy(
            cs.at[p], cr.at[p], sem_cs.at[n, p], sem_cr.at[n, p],
            device_id=partner, device_id_type=MESH,
        )

    def give_parts(n, left, right, shift):
        cs = (cs_a, cs_b)[n]

        def step(p):
            for half in range(2):
                value = part(left, right, shift, 2 * p + 1 - core, half)
                cs[p, pl.ds(half * 4, 4)] = value.astype(BF16).reshape(4, 96, F)
            core_copy(n, p).start()

        loop(2, step)

    def keep_parts(n, left, right, shift):
        own = (own_a, own_b)[n]

        def step(p):
            for half in range(2):
                value = part(left, right, shift, 2 * p + core, half)
                own[p, pl.ds(half * 4, 4)] = value.reshape(4, 96, F)

        loop(2, step)

    def push(n, src, dst, send, recv, mine, where, count):
        def step(r):
            t = (mine + 1 + r) % count
            pltpu.make_async_remote_copy(
                src.at[t] if n else src, dst.at[mine], send.at[t], recv.at[mine],
                device_id=where(t), device_id_type=MESH,
            ).start()

        loop(count - 1, step)

    def pushed(n, src, dst, send, recv, mine, where, count):
        def step(r):
            t = (mine + 1 + r) % count
            pltpu.make_async_remote_copy(
                src.at[t] if n else src, dst.at[mine], send.at[t], recv.at[mine],
                device_id=where(t), device_id_type=MESH,
            ).wait_send()

        loop(count - 1, step)

    def arrived(dst, recv, mine, count):
        def step(r):
            t = (mine + 1 + r) % count
            pltpu.make_async_copy(dst.at[t], dst.at[t], recv.at[t]).wait()

        loop(count - 1, step)

    back_act(c, pb, nv[2:3], 1, pr_b, sl_b, rh_b, 2)
    turn(c, 0, lt_b, 1)
    give_parts(1, lt_b, rh_b, 1)
    back_in(c, wb, 1, rh_b, gs)
    back_act(gs, pa, nv[0:1], 2, pr_a, sl_a, rh_a, 0)
    nb_core = pltpu.make_async_remote_copy(
        nbs, nbc, snc, rnc, device_id=partner, device_id_type=MESH
    )
    nb_core.start()
    back_in(gs, wa, 2, rh_a, gi)

    def send_out(j):
        q = cls + NC * j
        home = q // NB
        slot = q % NB

        @pl.when(home != d)
        def _():
            pltpu.make_async_remote_copy(
                gi.at[j], out.at[slot], so.at[j], ro.at[slot],
                device_id={"seq": home, "chrom": k}, device_id_type=MESH,
            ).start()

        @pl.when(home == d)
        def _():
            pltpu.make_async_copy(gi.at[j], out.at[slot], ro.at[slot]).start()

    loop(NB, send_out)

    turn(gs, 0, lt_a, 1)
    give_parts(0, lt_a, rh_a, 2)
    keep_parts(1, lt_b, rh_b, 1)

    def join_b(p):
        core_copy(1, p).wait_recv()
        for lo in range(2):
            for t in range(4):
                total = own_b[p, 4 * lo + t] + cr_b[p, 4 * lo + t].astype(F32)
                b1s[t, 2 * p + lo] = total.astype(BF16)

    def join_a(p):
        core_copy(0, p).wait_recv()
        for lo in range(2):
            for t in range(4):
                total = own_a[p, 4 * lo + t] + cr_a[p, 4 * lo + t].astype(F32)
                a1s[2 * p + lo, t] = total.astype(BF16)

    loop(2, join_b)
    push(1, b1s, b1r, sb1, rb1, y, to_y, 4)
    keep_parts(0, lt_a, rh_a, 2)
    nb_core.wait_recv()
    nb_core.wait_send()
    nbs[...] += nbc[...]
    push(0, nbs, nbx, snx, rnx, x, to_x, 4)
    loop(2, join_a)
    push(1, a1s, a1r, sa1, ra1, x, to_x, 4)

    def total_of(src, recv, mine, slot):
        total = src[mine, slot].astype(F32)
        for r in range(1, 4):
            total = total + recv[(mine + r) % 4, slot].astype(F32)
        return total

    arrived(nbx, rnx, x, 4)
    pushed(0, nbs, nbx, snx, rnx, x, to_x, 4)
    for r in range(1, 4):
        nbs[...] += nbx[(x + r) % 4]
    push(0, nbs, nby, sny, rny, y, to_y, 4)

    arrived(b1r, rb1, y, 4)

    def second_b(t):
        b2s[t] = total_of(b1s, b1r, y, t).astype(BF16)

    loop(4, second_b)
    push(1, b2s, b2r, sb2, rb2, x, to_x, 4)

    arrived(nby, rny, y, 4)
    pushed(0, nbs, nby, sny, rny, y, to_y, 4)
    for r in range(1, 4):
        nbs[...] += nby[(y + r) % 4]
    push(0, nbs, nbz, snz, rnz, z, to_z, 8)

    arrived(a1r, ra1, x, 4)

    def second_a(t):
        a2s[t] = total_of(a1s, a1r, x, t).astype(BF16)

    loop(4, second_a)
    push(1, a2s, a2r, sa2, ra2, y, to_y, 4)

    def last_total(src, recv, mine):
        total = src[mine].astype(F32)
        for r in range(1, 4):
            total = total + recv[(mine + r) % 4].astype(F32)
        return total

    arrived(b2r, rb2, x, 4)
    red_a[96:104] = jnp.zeros((8, F), F32)
    red_b[96:104] = jnp.zeros((8, F), F32)
    red_b[0:96] = last_total(b2s, b2r, x)
    arrived(a2r, ra2, y, 4)
    red_a[0:96] = last_total(a2s, a2r, y)
    for t in range(8):
        zs[t, 0] = red_a[12 * t : 12 * t + 16].astype(BF16)
        zs[t, 1] = red_b[12 * t : 12 * t + 16].astype(BF16)
    push(1, zs, zr, sz, rz, z, to_z, 8)

    factor = 1.0 / math.sqrt(4 * NC * NB * RB)
    arrived(nbz, rnz, z, 8)
    pushed(0, nbs, nbz, snz, rnz, z, to_z, 8)
    for r in range(1, 8):
        nbs[...] += nbz[(z + r) % 8]
    gna[...] = nbs[0:2] * factor
    gnb[...] = nbs[2:4] * factor

    arrived(zr, rz, z, 8)
    for n in range(2):
        total = zs[z, n].astype(F32)
        for r in range(1, 8):
            total = total + zr[(z + r) % 8, n].astype(F32)
        fg[k, n] = total * factor

    def spread(r):
        t = (k + 1 + r) % 4
        return pltpu.make_async_remote_copy(
            fg.at[k], fg.at[k], sf.at[t], rf.at[k], device_id=to_k(t), device_id_type=MESH
        )

    loop(3, lambda r: spread(r).start())
    arrived(fg, rf, k, 4)
    for n, conv, point in ((0, gca, gpa), (1, gcb, gpb)):
        for t in range(3):
            conv[t] = fg[t, n, 0:12]
        point[...] = fg[3, n].T[:, 0:12]

    loop(NB, lambda i: pltpu.make_async_copy(feat.at[0], out.at[i], ro.at[i]).wait())

    def sent(i):
        target = device_of((first + i) % NC)
        home = home_of(i)

        @pl.when(target != d)
        def _():
            for src, send in ((feat, su), (cot, sc)):
                pltpu.make_async_remote_copy(
                    src.at[i], c.at[0], send.at[i], rc.at[0],
                    device_id={"seq": target, "chrom": k}, device_id_type=MESH,
                ).wait_send()

        @pl.when(home != d)
        def _():
            pltpu.make_async_remote_copy(
                gi.at[i], out.at[0], so.at[i], ro.at[0],
                device_id={"seq": home, "chrom": k}, device_id_type=MESH,
            ).wait_send()

    loop(NB, sent)
    for n in range(2):
        for p in range(2):
            core_copy(n, p).wait_send()
    pushed(1, b1s, b1r, sb1, rb1, y, to_y, 4)
    pushed(1, a1s, a1r, sa1, ra1, x, to_x, 4)
    pushed(1, b2s, b2r, sb2, rb2, x, to_x, 4)
    pushed(1, a2s, a2r, sa2, ra2, y, to_y, 4)
    pushed(1, zs, zr, sz, rz, z, to_z, 8)
    loop(3, lambda r: spread(r).wait_send())


def body(feat, wa, sa, ba, pa, wb, sb, bb, pb, cot):
    feat = feat.reshape(NB, RB, C)
    cot = cot.reshape(NB, RB, C)
    vectors = [v.reshape(1, F) for v in (sa, ba, sb, bb)]
    hbm = pl.BlockSpec(memory_space=pltpu.HBM)
    vmem = pl.BlockSpec(memory_space=pltpu.VMEM)
    dma = pltpu.SemaphoreType.DMA

    def blocks(count, width=C):
        return pltpu.VMEM((count, RB, width), BF16)

    scratch = [
        blocks(NB + 4), blocks(NB), blocks(NB + 2), blocks(NB), blocks(NB),
        pltpu.VMEM((2, 320, F), F32), pltpu.VMEM((2, 320, F), F32),
        pltpu.VMEM((2, 320, F), F32), pltpu.VMEM((2, 320, F), F32),
        blocks(ACT + NB, F), blocks(ACT + NB, F),
        pltpu.VMEM((2, C, NB * RB), BF16), pltpu.VMEM((2, C, NB * RB), BF16),
        pltpu.VMEM((3, C, F), BF16), pltpu.VMEM((3, C, F), BF16),
        pltpu.VMEM((F, C), BF16), pltpu.VMEM((F, C), BF16), pltpu.VMEM((8, F), F32),
        pltpu.VMEM((2, 8, 96, F), F32), pltpu.VMEM((2, 8, 96, F), F32),
        pltpu.VMEM((2, 8, 96, F), BF16), pltpu.VMEM((2, 8, 96, F), BF16),
        pltpu.VMEM((2, 8, 96, F), BF16), pltpu.VMEM((2, 8, 96, F), BF16),
        pltpu.VMEM((4, 4, 96, F), BF16), pltpu.VMEM((4, 4, 96, F), BF16),
        pltpu.VMEM((4, 96, F), BF16), pltpu.VMEM((4, 96, F), BF16),
        pltpu.VMEM((4, 4, 96, F), BF16), pltpu.VMEM((4, 4, 96, F), BF16),
        pltpu.VMEM((4, 96, F), BF16), pltpu.VMEM((4, 96, F), BF16),
        pltpu.VMEM((104, F), F32), pltpu.VMEM((104, F), F32),
        pltpu.VMEM((8, 2, 16, F), BF16), pltpu.VMEM((8, 2, 16, F), BF16),
        pltpu.VMEM((4, 2, 16, F), F32),
        pltpu.VMEM((8, F), F32), pltpu.VMEM((8, F), F32), pltpu.VMEM((4, 8, F), F32),
        pltpu.VMEM((4, 8, F), F32), pltpu.VMEM((8, 8, F), F32),
        dma((8,)), dma((NB,)), dma((NB,)), dma((NB,)), dma((NB,)), dma((NB,)), dma((NB,)),
        dma((2, 2)), dma((2, 2)), dma((4,)), dma((4,)), dma((4,)), dma((4,)),
        dma((4,)), dma((4,)), dma((4,)), dma((4,)), dma((8,)), dma((8,)), dma((4,)), dma((4,)),
        dma, dma, dma((4,)), dma((4,)), dma((4,)), dma((4,)), dma((8,)), dma((8,)),
    ]
    shape = jax.ShapeDtypeStruct
    grad_in, gca, gpa, gna, gcb, gpb, gnb = pl.pallas_call(
        kernel,
        out_shape=[
            shape((NB, RB, C), BF16),
            shape((3, 12, F), F32), shape((F, 12), F32), shape((2, F), F32),
            shape((3, 12, F), F32), shape((F, 12), F32), shape((2, F), F32),
        ],
        in_specs=[hbm] * 10,
        out_specs=[hbm] + [vmem] * 6,
        scratch_shapes=scratch,
        compiler_params=pltpu.CompilerParams(
            collective_id=0, has_side_effects=True, vmem_limit_bytes=56 << 20
        ),
        cost_estimate=pl.CostEstimate(
            flops=23 * 2 * 640 * C * F, bytes_accessed=8 << 20, transcendentals=1 << 20
        ),
        name="blocks",
    )(feat, wa, vectors[0], vectors[1], pa, wb, vectors[2], vectors[3], pb, cot)
    return (
        grad_in.reshape(1, NB * RB, C), gca, gpa, gna[0], gna[1], gcb, gpb, gnb[0], gnb[1],
    )


def solution(mesh):
    bins = P("chrom", "seq", None)
    taps, projection = P(None, "seq", None), P(None, "seq")
    in_specs = (bins,) + (P(),) * 8 + (bins,)
    out_specs = (bins,) + (taps, projection, P(), P()) * 2
    return jax.shard_map(body, mesh=mesh, in_specs=in_specs, out_specs=out_specs, check_vma=False)
```

```python
import math

import jax
import jax.numpy as jnp
from jax import lax
from jax.experimental import pallas as pl
from jax.experimental.pallas import tpu as pltpu
from jax.sharding import PartitionSpec as P

MESH = pl.DeviceIdType.MESH
F32 = jnp.float32
BF16 = jnp.bfloat16
C = 768
F = 384
NB = 20
RB = 16
HALF = NB * RB
NC = 64
ACT = 24
STRIDE = 7


def device_of(c, core):
    g = (c // 4) % 8
    z = (g + jnp.where(g % 2 == 0, 1 + 2 * core, 7 - 2 * core)) % 8
    return (c // 32) * 32 + (c % 4) * 8 + z


def class_of(d, core):
    z = d % 8
    g = (z + jnp.where(z % 2 == 1, 7 - 2 * core, 1 + 2 * core)) % 8
    return (d // 32) * 32 + g * 4 + (d // 8) % 4


def dot(a, b):
    return jnp.dot(a, b, preferred_element_type=F32)


def dot_t(a, b):
    return lax.dot_general(a, b, (((1,), (1,)), ((), ())), preferred_element_type=F32)


def rows(ref, h, start):
    value = ref[h, pl.ds(start, NB)]
    return value.reshape(HALF, value.shape[-1])


def loop(n, step):
    def run(i, carry):
        step(i)
        return carry

    lax.fori_loop(0, n, run, 0)


def kernel(
    feat, wa_h, sa_h, ba_h, pa_h, wb_h, sb_h, bb_h, pb_h, cot,
    out, fin, norms,
    u, c, s, gs, gi, sl_a, sl_b, pr_a, pr_b, rh_a, rh_b, lt_a, lt_b,
    wa, wb, pa, pb, sa, ba, sb, bb,
    own_a, own_b, giv_a, giv_b, cs, cr,
    x1s, x1r, y1s, y1r, y2s, y2r, x2s, x2r, red, zs, zr, fg,
    nbs, nbc, nbx, nby, nbz,
    sem_w, su, ru, sc, rc, so, ro,
    sem_cs, sem_cr, sx1, rx1, sy1, ry1, sy2, ry2, sx2, rx2, sz, rz, sf, rf,
    snc, rnc, snx, rnx, sny, rny, snz, rnz,
):
    d = lax.axis_index("seq")
    k = lax.axis_index("chrom")
    xlo, y, z = d // 32, (d // 8) % 4, d % 8
    xhi, core = k // 2, k % 2
    x = 2 * xhi + xlo
    cls = class_of(d, core)
    first = NB * d

    def home_of(j):
        return (cls + NC * j) // NB

    def target_of(i):
        return device_of((first + i) % NC, core)

    def to_x(t):
        return {"seq": (t % 2) * 32 + d % 32, "chrom": 2 * (t // 2) + core}

    def to_y(t):
        return {"seq": xlo * 32 + t * 8 + z, "chrom": k}

    def to_z(t):
        return {"seq": xlo * 32 + y * 8 + t, "chrom": k}

    def to_k(t):
        return {"seq": d, "chrom": t}

    def to_seq(t):
        return {"seq": t, "chrom": k}

    partner = to_k(2 * xhi + 1 - core)

    def remote(src, dst, send, recv, where):
        return pltpu.make_async_remote_copy(
            src, dst, send, recv, device_id=where, device_id_type=MESH
        )

    barrier = pltpu.get_barrier_semaphore()

    def greet(where):
        pl.semaphore_signal(barrier, inc=1, device_id=where, device_id_type=MESH)

    def greet_block(i, count):
        home, target = home_of(i), target_of(i)

        @pl.when(home != d)
        def _():
            greet(to_seq(home))

        @pl.when(target != d)
        def _():
            greet(to_seq(target))

        return count + jnp.where(home != d, 1, 0) + jnp.where(target != d, 1, 0)

    greeted = lax.fori_loop(0, NB, greet_block, 0)
    for r in range(1, 4):
        greet(to_x((x + r) % 4))
        greet(to_y((y + r) % 4))
        greet(to_k((k + r) % 4))
    for r in range(1, 8):
        greet(to_z((z + r) % 8))
    pl.semaphore_wait(barrier, greeted + 16)

    def send_u(n):
        i = (n * STRIDE) % NB
        target, slot = target_of(i), (first + i) // NC

        @pl.when(target != d)
        def _():
            remote(feat.at[i], u.at[:, slot + 2], su.at[i], ru.at[slot], to_seq(target)).start()

        @pl.when(target == d)
        def _():
            pltpu.make_async_copy(feat.at[i], u.at[:, slot + 2], ru.at[slot]).start()

    def send_c(h):
        def step(n):
            i = (n * STRIDE) % NB
            target, slot = target_of(i), (first + i) // NC

            @pl.when(target != d)
            def _():
                remote(
                    cot.at[i, h], c.at[h, slot], sc.at[h, i], rc.at[h, slot], to_seq(target)
                ).start()

            @pl.when(target == d)
            def _():
                pltpu.make_async_copy(cot.at[i, h], c.at[h, slot], rc.at[h, slot]).start()

        loop(NB, step)

    loop(NB, send_u)
    loads = [
        (wa_h, wa), (wb_h, wb), (pa_h, pa), (pb_h, pb),
        (sa_h, sa), (ba_h, ba), (sb_h, sb), (bb_h, bb),
    ]
    loads = [pltpu.make_async_copy(a, b, sem_w.at[n]) for n, (a, b) in enumerate(loads)]
    for load in loads:
        load.start()
    send_c(0)
    send_c(1)

    for ref, count in ((u, 2), (s, 1), (rh_a, 2), (rh_b, 1)):
        zero = jnp.zeros((2, count) + ref.shape[2:], BF16)
        ref[:, pl.ds(0, count)] = zero
        ref[:, pl.ds(NB + count, count)] = zero
    nbs[...] = jnp.zeros_like(nbs)
    for load in loads:
        load.wait()

    loop(NB, lambda j: pltpu.make_async_copy(feat.at[0], u.at[:, j + 2], ru.at[j]).wait())

    def turn(src, pad, dst, which, h):
        dst[which, h] = rows(src, h, pad).T

    def ahead(src, shift, w, scale, offset, pre_ref, slope_ref, right):
        def step(h):
            pre = dot(rows(src, h, 0), w[0])
            pre = pre + dot(rows(src, h, shift), w[1])
            pre = pre + dot(rows(src, h, 2 * shift), w[2])
            normed = scale[...] * pre + offset[...]
            q = jax.nn.sigmoid(1.702 * normed)
            act = (normed * q).astype(BF16)
            pre_ref[h] = pre
            slope_ref[h] = q * (1.0 + 1.702 * normed * (1.0 - q))
            right[h, pl.ds(ACT, NB)] = act.reshape(NB, RB, F)
            if shift == 2:
                second = rows(src, h, 2).astype(F32) + dot(act, pa[...])
                s[h, pl.ds(1, NB)] = second.astype(BF16).reshape(NB, RB, C)

        loop(2, step)

    ahead(u, 2, wa, sa, ba, pr_a, sl_a, rh_a)
    ahead(s, 1, wb, sb, bb, pr_b, sl_b, rh_b)
    for h in range(2):
        turn(u, 2, lt_a, 0, h)
        turn(s, 1, lt_b, 0, h)

    def back_act(grad, p, scale, shift, pre_ref, slope_ref, right, row, h):
        grad_norm = dot_t(rows(grad, h, 0), p[...]) * slope_ref[h]
        right[h, pl.ds(shift, NB)] = (grad_norm * scale[...]).astype(BF16).reshape(NB, RB, F)
        nbs[row : row + 1] += jnp.sum(grad_norm * pre_ref[h], 0, keepdims=True)
        nbs[row + 1 : row + 2] += jnp.sum(grad_norm, 0, keepdims=True)

    def back_in(grad, w, shift, right, dst, h):
        total = rows(grad, h, 0).astype(F32)
        total = total + dot_t(rows(right, h, shift), w[1])
        total = total + dot_t(rows(right, h, 2 * shift), w[0])
        total = total + dot_t(rows(right, h, 0), w[2])
        dst[h] = total.astype(BF16).reshape(NB, RB, C)

    blocks = ((lt_a, rh_a, 2, own_a, giv_a), (lt_b, rh_b, 1, own_b, giv_b))

    def part(n, t, half, h):
        left, right, shift = blocks[n][:3]
        start = jnp.where(t == 3, ACT, 2 * shift - shift * t)
        value = dot(left[t // 3, h, pl.ds(half * 384, 384), :], rows(right, h, start))
        return value.reshape(4, 96, F)

    def core_copy(n, p):
        return remote(cs.at[n, p], cr.at[n, p], sem_cs.at[n, p], sem_cr.at[n, p], partner)

    def early_parts(n):
        own, giv = blocks[n][3:]

        def step(p):
            for half in range(2):
                giv[p, pl.ds(half * 4, 4)] = part(n, 2 * p + 1 - core, half, 0)
                own[p, pl.ds(half * 4, 4)] = part(n, 2 * p + core, half, 0)

        loop(2, step)

    def give_parts(n):
        giv = blocks[n][4]

        def step(p):
            for half in range(2):
                at = pl.ds(half * 4, 4)
                value = giv[p, at] + part(n, 2 * p + 1 - core, half, 1)
                cs[n, p, at] = value.astype(BF16)
            core_copy(n, p).start()

        loop(2, step)

    def keep_parts(n):
        own = blocks[n][3]

        def step(p):
            for half in range(2):
                at = pl.ds(half * 4, 4)
                own[p, at] += part(n, 2 * p + core, half, 1)

        loop(2, step)

    def exchange(src, dst, send, recv, mine, where, count, whole=False):
        def copy(r):
            t = (mine + 1 + r) % count
            return remote(src if whole else src.at[t], dst.at[mine], send.at[t], recv.at[mine], where(t))

        def arrive(r):
            t = (mine + 1 + r) % count
            pltpu.make_async_copy(dst.at[t], dst.at[t], recv.at[t]).wait()

        return (
            lambda: loop(count - 1, lambda r: copy(r).start()),
            lambda: loop(count - 1, arrive),
            lambda: loop(count - 1, lambda r: copy(r).wait_send()),
        )

    xs1 = [exchange(x1s.at[n], x1r.at[n], sx1.at[n], rx1.at[n], x, to_x, 4) for n in range(2)]
    ys1 = [exchange(y1s.at[n], y1r.at[n], sy1.at[n], ry1.at[n], y, to_y, 4) for n in range(2)]
    ys2 = [exchange(y2s.at[n], y2r.at[n], sy2.at[n], ry2.at[n], y, to_y, 4) for n in range(2)]
    xs2 = [exchange(x2s.at[n], x2r.at[n], sx2.at[n], rx2.at[n], x, to_x, 4) for n in range(2)]
    zs3 = [exchange(zs.at[n], zr.at[n], sz.at[n], rz.at[n], z, to_z, 8) for n in range(2)]
    nx = exchange(nbs, nbx, snx, rnx, x, to_x, 4, whole=True)
    ny = exchange(nbs, nby, sny, rny, y, to_y, 4, whole=True)
    nz = exchange(nbs, nbz, snz, rnz, z, to_z, 8, whole=True)

    def join(n):
        own = blocks[n][3]

        def step(p):
            core_copy(n, p).wait_recv()
            for lo in range(2):
                for t in range(4):
                    total = (own[p, 4 * lo + t] + cr[n, p, 4 * lo + t].astype(F32)).astype(BF16)
                    x1s[n, 2 * p + lo, t] = total[0:48]
                    y1s[n, t, 2 * p + lo] = total[48:96]

        loop(2, step)
        xs1[n][0]()
        ys1[n][0]()

    def total_of(src, recv, mine, slot):
        total = src[mine, slot].astype(F32)
        for r in range(1, 4):
            total = total + recv[(mine + r) % 4, slot].astype(F32)
        return total

    def second_step(n):
        xs1[n][1]()

        def lower(t):
            y2s[n, t] = total_of(x1s.at[n], x1r.at[n], x, t).astype(BF16)

        loop(4, lower)
        ys2[n][0]()
        ys1[n][1]()

        def upper(t):
            x2s[n, t] = total_of(y1s.at[n], y1r.at[n], y, t).astype(BF16)

        loop(4, upper)
        xs2[n][0]()

    def last_total(src, recv, mine):
        total = src[mine].astype(F32)
        for r in range(1, 4):
            total = total + recv[(mine + r) % 4].astype(F32)
        return total

    def third_step(n):
        ys2[n][1]()
        red[n, 0:48] = last_total(y2s.at[n], y2r.at[n], y)
        xs2[n][1]()
        red[n, 48:96] = last_total(x2s.at[n], x2r.at[n], x)
        for t in range(8):
            zs[n, t] = red[n, 12 * t : 12 * t + 16].astype(BF16)
        zs3[n][0]()

    factor = 1.0 / math.sqrt(4 * NC * NB * 2 * RB)

    def spread(n, r):
        t = (k + 1 + r) % 4
        return remote(fg.at[n, k], fg.at[n, k], sf.at[n, t], rf.at[n, k], to_k(t))

    def last_step(n):
        zs3[n][1]()
        total = zs[n, z].astype(F32)
        for r in range(1, 8):
            total = total + zr[n, (z + r) % 8].astype(F32)
        fg[n, k] = total * factor
        loop(3, lambda r: spread(n, r).start())

    def send_out(h):
        def step(m):
            j = (m * STRIDE) % NB
            home, slot = home_of(j), (cls + NC * j) % NB

            @pl.when(home != d)
            def _():
                remote(
                    gi.at[h, j], out.at[slot, h], so.at[h, j], ro.at[h, slot], to_seq(home)
                ).start()

            @pl.when(home == d)
            def _():
                pltpu.make_async_copy(gi.at[h, j], out.at[slot, h], ro.at[h, slot]).start()

        loop(NB, step)

    def wait_c(h):
        loop(NB, lambda j: pltpu.make_async_copy(cot.at[0, h], c.at[h, j], rc.at[h, j]).wait())

    red[:, 96:104] = jnp.zeros((2, 8, F), F32)

    wait_c(0)
    back_act(c, pb, sb, 1, pr_b, sl_b, rh_b, 2, 0)
    turn(c, 0, lt_b, 1, 0)
    back_in(c, wb, 1, rh_b, gs, 0)
    back_act(gs, pa, sa, 2, pr_a, sl_a, rh_a, 0, 0)
    back_in(gs, wa, 2, rh_a, gi, 0)
    turn(gs, 0, lt_a, 1, 0)
    early_parts(1)
    early_parts(0)

    wait_c(1)
    send_out(0)
    back_act(c, pb, sb, 1, pr_b, sl_b, rh_b, 2, 1)
    turn(c, 0, lt_b, 1, 1)
    give_parts(1)
    back_in(c, wb, 1, rh_b, gs, 1)
    back_act(gs, pa, sa, 2, pr_a, sl_a, rh_a, 0, 1)
    nb_core = remote(nbs, nbc, snc, rnc, partner)
    nb_core.start()
    keep_parts(1)
    join(1)
    back_in(gs, wa, 2, rh_a, gi, 1)
    send_out(1)
    turn(gs, 0, lt_a, 1, 1)
    give_parts(0)
    nb_core.wait()
    nbs[...] += nbc[...]
    nx[0]()
    keep_parts(0)
    join(0)
    second_step(1)

    def norm_sum(step, arrived, mine, count):
        step[1]()
        step[2]()
        for r in range(1, count):
            nbs[...] += arrived[(mine + r) % count]

    norm_sum(nx, nbx, x, 4)
    ny[0]()
    third_step(1)
    norm_sum(ny, nby, y, 4)
    nz[0]()
    second_step(0)
    last_step(1)
    norm_sum(nz, nbz, z, 8)
    norms[...] = nbs[...] * factor
    third_step(0)
    last_step(0)

    for h in range(2):
        loop(NB, lambda i: pltpu.make_async_copy(cot.at[0, h], out.at[i, h], ro.at[h, i]).wait())

    def sent(i):
        home, target = home_of(i), target_of(i)

        @pl.when(target != d)
        def _():
            remote(feat.at[i], u.at[:, 0], su.at[i], ru.at[0], to_seq(target)).wait_send()
            for h in range(2):
                remote(cot.at[i, h], c.at[h, 0], sc.at[h, i], rc.at[h, 0], to_seq(target)).wait_send()

        @pl.when(home != d)
        def _():
            for h in range(2):
                remote(gi.at[h, i], out.at[0, h], so.at[h, i], ro.at[h, 0], to_seq(home)).wait_send()

    loop(NB, sent)
    for n in range(2):
        for p in range(2):
            core_copy(n, p).wait_send()
        for step in (xs1, ys1, ys2, xs2, zs3):
            step[n][2]()
    for n in range(2):
        for r in range(3):
            t = (k + 1 + r) % 4
            pltpu.make_async_copy(fg.at[n, t], fg.at[n, t], rf.at[n, t]).wait()
            spread(n, r).wait_send()
    fin[...] = fg[...]


def finish(grad, fin, norms, out, gca, gpa, gsa, gba, gcb, gpb, gsb, gbb, held, ins, outs):
    parts = 4
    each = grad.shape[0] // parts
    at = [pl.ds(n * each, each) for n in range(parts)]
    into = [pltpu.make_async_copy(grad.at[at[n]], held.at[at[n]], ins.at[n]) for n in range(parts)]
    onto = [pltpu.make_async_copy(held.at[at[n]], out.at[at[n]], outs.at[n]) for n in range(parts)]
    for copy in into:
        copy.start()
    for n in range(parts):
        into[n].wait()
        onto[n].start()
    for n, conv, point, scale, offset in ((0, gca, gpa, gsa, gba), (1, gcb, gpb, gsb, gbb)):
        for t in range(3):
            conv[t] = fin[n, t, 0:12]
        point[...] = fin[n, 3, 0:12]
        scale[...] = norms[2 * n]
        offset[...] = norms[2 * n + 1]
    for copy in onto:
        copy.wait()


def body(feat, wa, sa, ba, pa, wb, sb, bb, pb, cot):
    feat = feat.reshape(NB, 2, RB, C)
    cot = cot.reshape(NB, 2, RB, C)
    hbm = pl.BlockSpec(memory_space=pltpu.HBM)
    vmem = pl.BlockSpec(memory_space=pltpu.VMEM)
    dma = pltpu.SemaphoreType.DMA

    def bins(count, width=C):
        return pltpu.VMEM((2, count, RB, width), BF16)

    def terms(*dims):
        return pltpu.VMEM((2,) + dims + (F,), BF16)

    flat = pltpu.VMEM((2, HALF, F), F32)
    whole = pltpu.VMEM((2, 8, 96, F), F32)
    turned = pltpu.VMEM((2, 2, C, HALF), BF16)
    scratch = (
        [bins(NB + 4), bins(NB), bins(NB + 2), bins(NB), bins(NB)]
        + [flat] * 4
        + [bins(ACT + NB, F)] * 2
        + [turned] * 2
        + [pltpu.VMEM((3, C, F), BF16)] * 2
        + [pltpu.VMEM((F, C), BF16)] * 2
        + [pltpu.VMEM((F,), F32)] * 4
        + [whole] * 4
        + [terms(2, 8, 96)] * 2
        + [terms(4, 4, 48)] * 4
        + [terms(4, 48)] * 4
        + [pltpu.VMEM((2, 104, F), F32)]
        + [terms(8, 16)] * 2
        + [pltpu.VMEM((2, 4, 16, F), F32)]
        + [pltpu.VMEM((8, F), F32)] * 2
        + [pltpu.VMEM((4, 8, F), F32)] * 2
        + [pltpu.VMEM((8, 8, F), F32)]
        + [dma((8,)), dma((NB,)), dma((NB,))]
        + [dma((2, NB))] * 4
        + [dma((2, 2))] * 2
        + [dma((2, 4))] * 8
        + [dma((2, 8))] * 2
        + [dma((2, 4))] * 2
        + [dma] * 2
        + [dma((4,))] * 4
        + [dma((8,))] * 2
    )
    shape = jax.ShapeDtypeStruct
    grad, fin, norms = pl.pallas_call(
        kernel,
        out_shape=[shape((NB, 2, RB, C), BF16), shape((2, 4, 16, F), F32), shape((8, F), F32)],
        in_specs=[hbm] * 10,
        out_specs=[hbm, vmem, vmem],
        scratch_shapes=scratch,
        compiler_params=pltpu.CompilerParams(
            collective_id=0, has_side_effects=True, vmem_limit_bytes=58 << 20
        ),
        cost_estimate=pl.CostEstimate(
            flops=23 * 2 * 640 * C * F, bytes_accessed=8 << 20, transcendentals=1 << 20
        ),
        name="blocks",
    )(feat, wa, sa, ba, pa, wb, sb, bb, pb, cot)
    small = [shape((3, 12, F), F32), shape((12, F), F32), shape((F,), F32), shape((F,), F32)]
    grad, gca, gpa, gsa, gba, gcb, gpb, gsb, gbb = pl.pallas_call(
        finish,
        out_shape=[shape((NB * 2 * RB, C), BF16)] + small * 2,
        in_specs=[hbm, vmem, vmem],
        out_specs=[hbm] + [vmem] * 8,
        scratch_shapes=[pltpu.VMEM((NB * 2 * RB, C), BF16), dma((4,)), dma((4,))],
        name="finish",
    )(grad.reshape(NB * 2 * RB, C), fin, norms)
    return (grad[None], gca, gpa.T, gsa, gba, gcb, gpb.T, gsb, gbb)


def solution(mesh):
    bins = P("chrom", "seq", None)
    taps, projection = P(None, "seq", None), P(None, "seq")
    in_specs = (bins,) + (P(),) * 8 + (bins,)
    out_specs = (bins,) + (taps, projection, P(), P()) * 2
    return jax.shard_map(body, mesh=mesh, in_specs=in_specs, out_specs=out_specs, check_vma=False)
```

```python
import math

import jax
import jax.numpy as jnp
from jax import lax
from jax.experimental import pallas as pl
from jax.experimental.pallas import tpu as pltpu
from jax.sharding import PartitionSpec as P

MESH = pl.DeviceIdType.MESH
F32 = jnp.float32
BF16 = jnp.bfloat16
C = 768
F = 384
NB = 20
RB = 16
HALF = NB * RB
NC = 64
ACT = 24
STRIDE = 7


def device_of(c, core):
    g = lax.rem(lax.div(c, 4), 8)
    z = lax.rem(g + jnp.where(lax.rem(g, 2) == 0, 1 + 2 * core, 7 - 2 * core), 8)
    return lax.div(c, 32) * 32 + lax.rem(c, 4) * 8 + z


def class_of(d, core):
    z = lax.rem(d, 8)
    g = lax.rem(z + jnp.where(lax.rem(z, 2) == 1, 7 - 2 * core, 1 + 2 * core), 8)
    return lax.div(d, 32) * 32 + g * 4 + lax.rem(lax.div(d, 8), 4)


def tile(row):
    return pl.multiple_of(row, 16)


def split(value):
    high = value.astype(BF16).astype(F32)
    return jnp.concatenate([high, value - high], 0).astype(BF16)


def dot(a, b):
    return jnp.dot(a, b, preferred_element_type=F32)


def dot_t(a, b):
    return lax.dot_general(a, b, (((1,), (1,)), ((), ())), preferred_element_type=F32)


def rows(ref, h, start):
    value = ref[h, pl.ds(start, NB)]
    return value.reshape(HALF, value.shape[-1])


def loop(n, step):
    def run(i, carry):
        step(i)
        return carry

    lax.fori_loop(0, n, run, 0)


def kernel(
    feat, wa_h, sa_h, ba_h, pa_h, wb_h, sb_h, bb_h, pb_h, cot,
    out, fin, norms,
    u, c, s, gs, gi, sl_a, sl_b, pr_a, pr_b, rh_a, rh_b, lt_a, lt_b,
    wa, wb, pa, pb, sa, ba, sb, bb,
    own_a, own_b, giv_a, giv_b, cs, cr,
    x1s_a, x1r_a, x1s_b, x1r_b, y1s_a, y1r_a, y1s_b, y1r_b,
    y2s_a, y2r_a, y2s_b, y2r_b, x2s_a, x2r_a, x2s_b, x2r_b, red, zs, zr, fg, nbs, nbc,
    sem_w, su, ru, sc, rc, so, ro,
    sem_cs, sem_cr, sx1, rx1, sy1, ry1, sy2, ry2, sx2, rx2, sz, rz, sf, rf, snc, rnc,
):
    d = lax.axis_index("seq")
    k = lax.axis_index("chrom")
    xlo, y, z = lax.div(d, 32), lax.rem(lax.div(d, 8), 4), lax.rem(d, 8)
    xhi, core = lax.div(k, 2), lax.rem(k, 2)
    x = 2 * xhi + xlo
    cls = class_of(d, core)
    slot_0, class_0 = lax.div(NB * d, NC), lax.rem(NB * d, NC)

    def going(n, r):
        i = lax.rem(STRIDE * (5 * n + r), NB)
        c_ = class_0 + i
        over = jnp.where(c_ >= NC, 1, 0)
        return i, device_of(c_ - NC * over, core), slot_0 + over

    home_0, place_0 = lax.div(cls, NB), lax.rem(cls, NB)

    def coming(n, r):
        j = lax.rem(STRIDE * (5 * n + r), NB)
        n, r = lax.div(j, 5), lax.rem(j, 5)
        place = place_0 + 4 * r
        over = jnp.where(place >= NB, 1, 0)
        return j, home_0 + 16 * n + 3 * r + over, place - NB * over

    def to_x(t):
        return {"seq": lax.rem(t, 2) * 32 + 8 * y + z, "chrom": 2 * lax.div(t, 2) + core}

    def to_y(t):
        return {"seq": xlo * 32 + t * 8 + z, "chrom": k}

    def to_z(t):
        return {"seq": xlo * 32 + y * 8 + t, "chrom": k}

    def to_k(t):
        return {"seq": d, "chrom": t}

    def to_seq(t):
        return {"seq": t, "chrom": k}

    partner = to_k(2 * xhi + 1 - core)

    def remote(src, dst, send, recv, where):
        return pltpu.make_async_remote_copy(
            src, dst, send, recv, device_id=where, device_id_type=MESH
        )

    barrier = pltpu.get_barrier_semaphore()

    def greet(where):
        pl.semaphore_signal(barrier, inc=1, device_id=where, device_id_type=MESH)

    def greet_blocks(n, count):
        for r in range(5):
            for other in (going(n, r)[1], coming(n, r)[1]):

                @pl.when(other != d)
                def _():
                    greet(to_seq(other))

                count = count + jnp.where(other != d, 1, 0)
        return count

    greeted = lax.fori_loop(0, 4, greet_blocks, 0)
    for r in range(1, 4):
        greet(to_x(lax.rem(x + r, 4)))
        greet(to_y(lax.rem(y + r, 4)))
        greet(to_k(lax.rem(k + r, 4)))
    for r in range(1, 8):
        greet(to_z(lax.rem(z + r, 8)))
    pl.semaphore_wait(barrier, greeted + 16)

    def send_u(n):
        for r in range(5):
            i, target, slot = going(n, r)

            @pl.when(target != d)
            def _():
                remote(feat.at[i], u.at[:, slot + 2], su.at[i], ru.at[slot], to_seq(target)).start()

            @pl.when(target == d)
            def _():
                pltpu.make_async_copy(feat.at[i], u.at[:, slot + 2], ru.at[slot]).start()

    def send_c(h):
        def step(n):
            for r in range(5):
                i, target, slot = going(n, r)
                src, dst, recv = cot.at[i, h], c.at[h, slot], rc.at[h, slot]

                @pl.when(target != d)
                def _():
                    remote(src, dst, sc.at[h, i], recv, to_seq(target)).start()

                @pl.when(target == d)
                def _():
                    pltpu.make_async_copy(src, dst, recv).start()

        loop(4, step)

    loop(4, send_u)
    loads = [
        (wa_h, wa), (wb_h, wb), (pa_h, pa), (pb_h, pb),
        (sa_h, sa), (ba_h, ba), (sb_h, sb), (bb_h, bb),
    ]
    loads = [pltpu.make_async_copy(a, b, sem_w.at[n]) for n, (a, b) in enumerate(loads)]
    for load in loads:
        load.start()
    send_c(0)
    send_c(1)

    for ref, count in ((u, 2), (s, 1), (rh_a, 2), (rh_b, 1)):
        zero = jnp.zeros((2, count) + ref.shape[2:], BF16)
        ref[:, pl.ds(0, count)] = zero
        ref[:, pl.ds(NB + count, count)] = zero
    nbs[...] = jnp.zeros_like(nbs)
    for load in loads:
        load.wait()

    loop(NB, lambda j: pltpu.make_async_copy(feat.at[0], u.at[:, j + 2], ru.at[j]).wait())

    def turn(src, pad, dst, which, h):
        dst[which, h] = rows(src, h, pad).T

    def ahead(src, shift, w, scale, offset, pre_ref, slope_ref, right):
        def step(h):
            pre = dot(rows(src, h, 0), w[0])
            pre = pre + dot(rows(src, h, shift), w[1])
            pre = pre + dot(rows(src, h, 2 * shift), w[2])
            normed = scale[...] * pre + offset[...]
            q = jax.nn.sigmoid(1.702 * normed)
            act = (normed * q).astype(BF16)
            pre_ref[h] = pre
            slope_ref[h] = q * (1.0 + 1.702 * normed * (1.0 - q))
            right[h, pl.ds(ACT, NB)] = act.reshape(NB, RB, F)
            if shift == 2:
                second = rows(src, h, 2).astype(F32) + dot(act, pa[...])
                s[h, pl.ds(1, NB)] = second.astype(BF16).reshape(NB, RB, C)

        loop(2, step)

    ahead(u, 2, wa, sa, ba, pr_a, sl_a, rh_a)
    ahead(s, 1, wb, sb, bb, pr_b, sl_b, rh_b)
    for h in range(2):
        turn(u, 2, lt_a, 0, h)
        turn(s, 1, lt_b, 0, h)

    def back_act(grad, p, scale, shift, pre_ref, slope_ref, right, row, h):
        grad_norm = dot_t(rows(grad, h, 0), p[...]) * slope_ref[h]
        right[h, pl.ds(shift, NB)] = (grad_norm * scale[...]).astype(BF16).reshape(NB, RB, F)
        nbs[row : row + 1] += jnp.sum(grad_norm * pre_ref[h], 0, keepdims=True)
        nbs[row + 1 : row + 2] += jnp.sum(grad_norm, 0, keepdims=True)

    def back_in(grad, w, shift, right, dst, h):
        total = rows(grad, h, 0).astype(F32)
        total = total + dot_t(rows(right, h, shift), w[1])
        total = total + dot_t(rows(right, h, 2 * shift), w[0])
        total = total + dot_t(rows(right, h, 0), w[2])
        dst[h] = total.astype(BF16).reshape(NB, RB, C)

    blocks = ((lt_a, rh_a, 2, own_a, giv_a), (lt_b, rh_b, 1, own_b, giv_b))

    def part(n, t, half, h):
        left, right, shift = blocks[n][:3]
        start = jnp.where(t == 3, ACT, 2 * shift - shift * t)
        value = dot(left[t // 3, h, pl.ds(half * 384, 384), :], rows(right, h, start))
        return value.reshape(4, 96, F)

    def core_copy(n, p):
        return remote(cs.at[n, p], cr.at[n, p], sem_cs.at[n, p], sem_cr.at[n, p], partner)

    def early_parts(n):
        own, giv = blocks[n][3:]

        def step(p):
            for half in range(2):
                giv[p, pl.ds(half * 4, 4)] = part(n, 2 * p + 1 - core, half, 0)
                own[p, pl.ds(half * 4, 4)] = part(n, 2 * p + core, half, 0)

        loop(2, step)

    def give_parts(n):
        giv = blocks[n][4]

        def step(p):
            for half in range(2):
                at = pl.ds(half * 4, 4)
                value = giv[p, at] + part(n, 2 * p + 1 - core, half, 1)
                cs[n, p, at] = value.astype(BF16)
            core_copy(n, p).start()

        loop(2, step)

    def keep_parts(n):
        own = blocks[n][3]

        def step(p):
            for half in range(2):
                at = pl.ds(half * 4, 4)
                own[p, at] += part(n, 2 * p + core, half, 1)

        loop(2, step)

    def exchange(src, dst, send, recv, mine, where, count):
        def copy(r):
            t = lax.rem(mine + 1 + r, count)
            return remote(src.at[t], dst.at[mine], send.at[t], recv.at[mine], where(t))

        def arrive(r):
            t = lax.rem(mine + 1 + r, count)
            pltpu.make_async_copy(dst.at[t], dst.at[t], recv.at[t]).wait()

        return (
            lambda: loop(count - 1, lambda r: copy(r).start()),
            lambda: loop(count - 1, arrive),
            lambda: loop(count - 1, lambda r: copy(r).wait_send()),
        )

    x1s, x1r, y1s, y1r = (x1s_a, x1s_b), (x1r_a, x1r_b), (y1s_a, y1s_b), (y1r_a, y1r_b)
    y2s, y2r, x2s, x2r = (y2s_a, y2s_b), (y2r_a, y2r_b), (x2s_a, x2s_b), (x2r_a, x2r_b)
    xs1 = [exchange(x1s[n], x1r[n], sx1.at[n], rx1.at[n], x, to_x, 4) for n in range(2)]
    ys1 = [exchange(y1s[n], y1r[n], sy1.at[n], ry1.at[n], y, to_y, 4) for n in range(2)]
    ys2 = [exchange(y2s[n], y2r[n], sy2.at[n], ry2.at[n], y, to_y, 4) for n in range(2)]
    xs2 = [exchange(x2s[n], x2r[n], sx2.at[n], rx2.at[n], x, to_x, 4) for n in range(2)]
    zs3 = exchange(zs, zr, sz, rz, z, to_z, 8)
    nb_core = remote(nbs, nbc, snc, rnc, partner)

    def join(n):
        own = blocks[n][3]

        def step(p):
            core_copy(n, p).wait_recv()
            for lo in range(2):
                for t in range(4):
                    total = (own[p, 4 * lo + t] + cr[n, p, 4 * lo + t].astype(F32)).astype(BF16)
                    x1s[n][2 * p + lo, 48 * t : 48 * t + 48] = total[0:48]
                    y1s[n][t, pl.ds(tile(96 * p + 48 * lo), 48)] = total[48:96]

        if n == 0:
            nb_core.wait_recv()
            for t in range(4):
                x1s[n][t, 192:208] = split(nbs[...] + nbc[...])
        loop(2, step)
        xs1[n][0]()
        ys1[n][0]()

    def total_of(src, recv, mine, at, size, count=4):
        total = src[mine, pl.ds(at, size)].astype(F32)
        for r in range(1, count):
            total = total + recv[lax.rem(mine + r, count), pl.ds(at, size)].astype(F32)
        return total

    def norms_of(src, recv, mine, at, count=4):
        total = total_of(src, recv, mine, at, 16, count)
        return total[0:8] + total[8:16]

    def second_step(n):
        xs1[n][1]()

        def lower(t):
            y2s[n][t, 0:48] = total_of(x1s[n], x1r[n], x, tile(48 * t), 48).astype(BF16)
            if n == 0:
                y2s[n][t, 48:64] = split(norms_of(x1s[n], x1r[n], x, 192))

        loop(4, lower)
        ys2[n][0]()
        ys1[n][1]()

        def upper(t):
            x2s[n][t] = total_of(y1s[n], y1r[n], y, tile(48 * t), 48).astype(BF16)

        loop(4, upper)
        xs2[n][0]()

    def third_step(n):
        ys2[n][1]()
        red[n, 0:48] = total_of(y2s[n], y2r[n], y, 0, 48)
        if n == 0:
            some = split(norms_of(y2s[n], y2r[n], y, 48))
            for t in range(8):
                zs[t, 32:48] = some
        xs2[n][1]()
        red[n, 48:96] = total_of(x2s[n], x2r[n], x, 0, 48)
        for t in range(8):
            zs[t, 16 * n : 16 * n + 16] = red[n, 12 * t : 12 * t + 16].astype(BF16)

    factor = 1.0 / math.sqrt(4 * NC * NB * 2 * RB)

    def spread(r):
        t = lax.rem(k + 1 + r, 4)
        return remote(fg.at[k], fg.at[k], sf.at[t], rf.at[k], to_k(t))

    def send_out(h):
        def step(n):
            for r in range(5):
                j, home, place = coming(n, r)
                src, dst, recv = gi.at[h, j], out.at[place, h], ro.at[h, place]

                @pl.when(home != d)
                def _():
                    remote(src, dst, so.at[h, j], recv, to_seq(home)).start()

                @pl.when(home == d)
                def _():
                    pltpu.make_async_copy(src, dst, recv).start()

        loop(4, step)

    def wait_c(h):
        loop(NB, lambda j: pltpu.make_async_copy(cot.at[0, h], c.at[h, j], rc.at[h, j]).wait())

    red[:, 96:104] = jnp.zeros((2, 8, F), F32)

    wait_c(0)
    back_act(c, pb, sb, 1, pr_b, sl_b, rh_b, 2, 0)
    turn(c, 0, lt_b, 1, 0)
    back_in(c, wb, 1, rh_b, gs, 0)
    back_act(gs, pa, sa, 2, pr_a, sl_a, rh_a, 0, 0)
    back_in(gs, wa, 2, rh_a, gi, 0)
    turn(gs, 0, lt_a, 1, 0)
    early_parts(1)
    early_parts(0)

    wait_c(1)
    send_out(0)
    back_act(c, pb, sb, 1, pr_b, sl_b, rh_b, 2, 1)
    turn(c, 0, lt_b, 1, 1)
    give_parts(1)
    keep_parts(1)
    back_in(c, wb, 1, rh_b, gs, 1)
    join(1)
    back_act(gs, pa, sa, 2, pr_a, sl_a, rh_a, 0, 1)
    nb_core.start()
    turn(gs, 0, lt_a, 1, 1)
    give_parts(0)
    keep_parts(0)
    join(0)
    back_in(gs, wa, 2, rh_a, gi, 1)
    send_out(1)
    second_step(1)
    second_step(0)
    third_step(1)
    third_step(0)
    zs3[0]()
    zs3[1]()
    fg[k] = total_of(zs, zr, z, 0, 32, 8) * factor
    loop(3, lambda r: spread(r).start())
    norms[...] = norms_of(zs, zr, z, 32, 8) * factor
    for h in range(2):
        loop(NB, lambda i: pltpu.make_async_copy(cot.at[0, h], out.at[i, h], ro.at[h, i]).wait())

    def sent(n):
        for r in range(5):
            i, target, _ = going(n, r)
            j, home, _ = coming(n, r)

            @pl.when(target != d)
            def _():
                remote(feat.at[i], u.at[:, 0], su.at[i], ru.at[0], to_seq(target)).wait_send()
                for h in range(2):
                    remote(
                        cot.at[i, h], c.at[h, 0], sc.at[h, i], rc.at[h, 0], to_seq(target)
                    ).wait_send()

            @pl.when(home != d)
            def _():
                for h in range(2):
                    remote(
                        gi.at[h, j], out.at[0, h], so.at[h, j], ro.at[h, 0], to_seq(home)
                    ).wait_send()

    loop(4, sent)
    nb_core.wait_send()
    for n in range(2):
        for p in range(2):
            core_copy(n, p).wait_send()
        for step in (xs1, ys1, ys2, xs2):
            step[n][2]()
    zs3[2]()
    for r in range(3):
        t = lax.rem(k + 1 + r, 4)
        pltpu.make_async_copy(fg.at[t], fg.at[t], rf.at[t]).wait()
        spread(r).wait_send()
    fin[...] = fg[...]


def finish(grad, fin, norms, out, gca, gpa, gsa, gba, gcb, gpb, gsb, gbb, held, fv, nv, v0, v1, v2, v3, q0, q1, p0, p1, ins, outs):
    def copy(src, dst, sem):
        return pltpu.make_async_copy(src, dst, sem)

    parts = 4
    each = grad.shape[0] // parts
    at = [pl.ds(n * each, each) for n in range(parts)]
    into = [copy(norms, nv, ins.at[0]), copy(fin, fv, ins.at[1])]
    into += [copy(grad.at[at[n]], held.at[at[n]], ins.at[2 + n]) for n in range(parts)]
    onto = [copy(v, o, outs.at[n]) for n, (v, o) in enumerate(zip((v0, v1, v2, v3), (gsa, gba, gsb, gbb)))]
    onto += [copy(v, o, outs.at[4 + n]) for n, (v, o) in enumerate(zip((q0, q1, p0, p1), (gca, gcb, gpa, gpb)))]
    onto += [copy(held.at[at[n]], out.at[at[n]], outs.at[8 + n]) for n in range(parts)]
    for one in into:
        one.start()
    into[0].wait()
    for n, v in enumerate((v0, v1, v2, v3)):
        v[...] = nv[n]
        onto[n].start()
    into[1].wait()
    for n, (conv, point) in enumerate(((q0, p0), (q1, p1))):
        for t in range(3):
            conv[t] = fv[t, 16 * n : 16 * n + 12]
        point[...] = fv[3, 16 * n : 16 * n + 12]
    for n in range(4, 8):
        onto[n].start()
    for n in range(parts):
        into[2 + n].wait()
        onto[8 + n].start()
    for one in onto:
        one.wait()


def body(feat, wa, sa, ba, pa, wb, sb, bb, pb, cot):
    feat = feat.reshape(NB, 2, RB, C)
    cot = cot.reshape(NB, 2, RB, C)
    hbm = pl.BlockSpec(memory_space=pltpu.HBM)
    vmem = pl.BlockSpec(memory_space=pltpu.VMEM)
    dma = pltpu.SemaphoreType.DMA

    def bins(count, width=C):
        return pltpu.VMEM((2, count, RB, width), BF16)

    def terms(*dims):
        return pltpu.VMEM(dims + (F,), BF16)

    flat = pltpu.VMEM((2, HALF, F), F32)
    whole = pltpu.VMEM((2, 8, 96, F), F32)
    turned = pltpu.VMEM((2, 2, C, HALF), BF16)
    scratch = (
        [bins(NB + 4), bins(NB), bins(NB + 2), bins(NB), bins(NB)]
        + [flat] * 4
        + [bins(ACT + NB, F)] * 2
        + [turned] * 2
        + [pltpu.VMEM((3, C, F), BF16)] * 2
        + [pltpu.VMEM((F, C), BF16)] * 2
        + [pltpu.VMEM((F,), F32)] * 4
        + [whole] * 4
        + [terms(2, 2, 8, 96)] * 2
        + [terms(4, 208)] * 2
        + [terms(4, 192)] * 6
        + [terms(4, 64)] * 2
        + [terms(4, 48)] * 6
        + [pltpu.VMEM((2, 104, F), F32)]
        + [terms(8, 48)] * 2
        + [pltpu.VMEM((4, 32, F), F32)]
        + [pltpu.VMEM((8, F), F32)] * 2
        + [dma((8,)), dma((NB,)), dma((NB,))]
        + [dma((2, NB))] * 4
        + [dma((2, 2))] * 2
        + [dma((2, 4))] * 8
        + [dma((8,))] * 2
        + [dma((4,))] * 2
        + [dma] * 2
    )
    shape = jax.ShapeDtypeStruct
    grad, fin, norms = pl.pallas_call(
        kernel,
        out_shape=[shape((NB, 2, RB, C), BF16), shape((4, 32, F), F32), shape((8, F), F32)],
        in_specs=[hbm] * 10,
        out_specs=[hbm, vmem, vmem],
        scratch_shapes=scratch,
        compiler_params=pltpu.CompilerParams(
            collective_id=0, has_side_effects=True, vmem_limit_bytes=58 << 20
        ),
        cost_estimate=pl.CostEstimate(
            flops=23 * 2 * 640 * C * F, bytes_accessed=8 << 20, transcendentals=1 << 20
        ),
        name="blocks",
    )(feat, wa, sa, ba, pa, wb, sb, bb, pb, cot)
    small = [shape((3, 12, F), F32), shape((12, F), F32), shape((F,), F32), shape((F,), F32)]
    grad, gca, gpa, gsa, gba, gcb, gpb, gsb, gbb = pl.pallas_call(
        finish,
        out_shape=[shape((NB * 2 * RB, C), BF16)] + small * 2,
        in_specs=[hbm] * 3,
        out_specs=[hbm] * 9,
        scratch_shapes=[
            pltpu.VMEM((NB * 2 * RB, C), BF16), pltpu.VMEM((4, 32, F), F32), pltpu.VMEM((8, F), F32),
            *[pltpu.VMEM((F,), F32)] * 4, *[pltpu.VMEM((3, 12, F), F32)] * 2,
            *[pltpu.VMEM((12, F), F32)] * 2, dma((6,)), dma((12,)),
        ],
        name="finish",
    )(grad.reshape(NB * 2 * RB, C), fin, norms)
    return (grad[None], gca, gpa.T, gsa, gba, gcb, gpb.T, gsb, gbb)


def solution(mesh):
    bins = P("chrom", "seq", None)
    taps, projection = P(None, "seq", None), P(None, "seq")
    in_specs = (bins,) + (P(),) * 8 + (bins,)
    out_specs = (bins,) + (taps, projection, P(), P()) * 2
    return jax.shard_map(body, mesh=mesh, in_specs=in_specs, out_specs=out_specs, check_vma=False)
```

```python
import math

import jax
import jax.numpy as jnp
from jax import lax
from jax.experimental import pallas as pl
from jax.experimental.pallas import tpu as pltpu
from jax.sharding import PartitionSpec as P

MESH = pl.DeviceIdType.MESH
F32 = jnp.float32
BF16 = jnp.bfloat16
C = 768
F = 384
NB = 20
RB = 16
HALF = NB * RB
NC = 64
ACT = 24
STRIDE = 7


def device_of(c, core):
    g = lax.rem(lax.div(c, 4), 8)
    z = lax.rem(g + jnp.where(lax.rem(g, 2) == 0, 1 + 2 * core, 7 - 2 * core), 8)
    return lax.div(c, 32) * 32 + lax.rem(c, 4) * 8 + z


def class_of(d, core):
    z = lax.rem(d, 8)
    g = lax.rem(z + jnp.where(lax.rem(z, 2) == 1, 7 - 2 * core, 1 + 2 * core), 8)
    return lax.div(d, 32) * 32 + g * 4 + lax.rem(lax.div(d, 8), 4)


def tile(row):
    return pl.multiple_of(row, 16)


def split(value):
    high = value.astype(BF16).astype(F32)
    return jnp.concatenate([high, value - high], 0).astype(BF16)


def dot(a, b):
    return jnp.dot(a, b, preferred_element_type=F32)


def dot_t(a, b):
    return lax.dot_general(a, b, (((1,), (1,)), ((), ())), preferred_element_type=F32)


def rows(ref, h, start):
    value = ref[h, pl.ds(start, NB)]
    return value.reshape(HALF, value.shape[-1])


def loop(n, step):
    def run(i, carry):
        step(i)
        return carry

    lax.fori_loop(0, n, run, 0)


def kernel(
    feat, wa_h, sa_h, ba_h, pa_h, wb_h, sb_h, bb_h, pb_h, cot,
    out, fin, norms,
    u, c, s, gs, gi, sl_a, sl_b, pr_a, pr_b, rh_a, rh_b, lt_a, lt_b,
    wa, wb, pa, pb, sa, ba, sb, bb,
    own_a, own_b, giv_a, giv_b, cs, cr,
    x1s_a, x1r_a, x1s_b, x1r_b, y1s_a, y1r_a, y1s_b, y1r_b,
    y2s_a, y2r_a, y2s_b, y2r_b, x2s_a, x2r_a, x2s_b, x2r_b, red, zs, zr, fg, nbs, nbc,
    sem_w, su, ru, sc, rc, so, ro,
    sem_cs, sem_cr, sx1, rx1, sy1, ry1, sy2, ry2, sx2, rx2, sz, rz, sf, rf, snc, rnc,
):
    d = lax.axis_index("seq")
    k = lax.axis_index("chrom")
    xlo, y, z = lax.div(d, 32), lax.rem(lax.div(d, 8), 4), lax.rem(d, 8)
    xhi, core = lax.div(k, 2), lax.rem(k, 2)
    x = 2 * xhi + xlo
    cls = class_of(d, core)
    slot_0, class_0 = lax.div(NB * d, NC), lax.rem(NB * d, NC)

    def going(n, r):
        i = lax.rem(STRIDE * (5 * n + r), NB)
        c_ = class_0 + i
        over = jnp.where(c_ >= NC, 1, 0)
        return i, device_of(c_ - NC * over, core), slot_0 + over

    home_0, place_0 = lax.div(cls, NB), lax.rem(cls, NB)

    def coming(n, r):
        j = lax.rem(STRIDE * (5 * n + r), NB)
        n, r = lax.div(j, 5), lax.rem(j, 5)
        place = place_0 + 4 * r
        over = jnp.where(place >= NB, 1, 0)
        return j, home_0 + 16 * n + 3 * r + over, place - NB * over

    def to_x(t):
        return {"seq": lax.rem(t, 2) * 32 + 8 * y + z, "chrom": 2 * lax.div(t, 2) + core}

    def to_y(t):
        return {"seq": xlo * 32 + t * 8 + z, "chrom": k}

    def to_z(t):
        return {"seq": xlo * 32 + y * 8 + t, "chrom": k}

    def to_k(t):
        return {"seq": d, "chrom": t}

    def to_seq(t):
        return {"seq": t, "chrom": k}

    partner = to_k(2 * xhi + 1 - core)

    def remote(src, dst, send, recv, where):
        return pltpu.make_async_remote_copy(
            src, dst, send, recv, device_id=where, device_id_type=MESH
        )

    barrier = pltpu.get_barrier_semaphore()

    def greet(where):
        pl.semaphore_signal(barrier, inc=1, device_id=where, device_id_type=MESH)

    def greet_blocks(n, count):
        for r in range(5):
            for other in (going(n, r)[1], coming(n, r)[1]):

                @pl.when(other != d)
                def _():
                    greet(to_seq(other))

                count = count + jnp.where(other != d, 1, 0)
        return count

    greeted = lax.fori_loop(0, 4, greet_blocks, 0)
    for r in range(1, 4):
        greet(to_x(lax.rem(x + r, 4)))
        greet(to_y(lax.rem(y + r, 4)))
        greet(to_k(lax.rem(k + r, 4)))
    for r in range(1, 8):
        greet(to_z(lax.rem(z + r, 8)))
    pl.semaphore_wait(barrier, greeted + 16)

    def send_u(n):
        for r in range(5):
            i, target, slot = going(n, r)

            @pl.when(target != d)
            def _():
                remote(feat.at[i], u.at[:, slot + 2], su.at[i], ru.at[slot], to_seq(target)).start()

            @pl.when(target == d)
            def _():
                pltpu.make_async_copy(feat.at[i], u.at[:, slot + 2], ru.at[slot]).start()

    def send_c(h):
        def step(n):
            for r in range(5):
                i, target, slot = going(n, r)
                src, dst, recv = cot.at[i, h], c.at[h, slot], rc.at[h, slot]

                @pl.when(target != d)
                def _():
                    remote(src, dst, sc.at[h, i], recv, to_seq(target)).start()

                @pl.when(target == d)
                def _():
                    pltpu.make_async_copy(src, dst, recv).start()

        loop(4, step)

    loop(4, send_u)
    loads = [
        (wa_h, wa), (wb_h, wb), (pa_h, pa), (pb_h, pb),
        (sa_h, sa), (ba_h, ba), (sb_h, sb), (bb_h, bb),
    ]
    loads = [pltpu.make_async_copy(a, b, sem_w.at[n]) for n, (a, b) in enumerate(loads)]
    for load in loads:
        load.start()
    send_c(0)
    send_c(1)

    for ref, count in ((u, 2), (s, 1), (rh_a, 2), (rh_b, 1)):
        zero = jnp.zeros((2, count) + ref.shape[2:], BF16)
        ref[:, pl.ds(0, count)] = zero
        ref[:, pl.ds(NB + count, count)] = zero
    nbs[...] = jnp.zeros_like(nbs)
    for load in loads:
        load.wait()

    loop(NB, lambda j: pltpu.make_async_copy(feat.at[0], u.at[:, j + 2], ru.at[j]).wait())

    def turn(src, pad, dst, which, h):
        dst[which, h] = rows(src, h, pad).T

    def ahead(src, shift, w, scale, offset, pre_ref, slope_ref, right):
        def step(h):
            pre = dot(rows(src, h, 0), w[0])
            pre = pre + dot(rows(src, h, shift), w[1])
            pre = pre + dot(rows(src, h, 2 * shift), w[2])
            normed = scale[...] * pre + offset[...]
            q = jax.nn.sigmoid(1.702 * normed)
            act = (normed * q).astype(BF16)
            pre_ref[h] = pre
            slope_ref[h] = q * (1.0 + 1.702 * normed * (1.0 - q))
            right[h, pl.ds(ACT, NB)] = act.reshape(NB, RB, F)
            if shift == 2:
                second = rows(src, h, 2).astype(F32) + dot(act, pa[...])
                s[h, pl.ds(1, NB)] = second.astype(BF16).reshape(NB, RB, C)

        loop(2, step)

    ahead(u, 2, wa, sa, ba, pr_a, sl_a, rh_a)
    ahead(s, 1, wb, sb, bb, pr_b, sl_b, rh_b)
    for h in range(2):
        turn(u, 2, lt_a, 0, h)
        turn(s, 1, lt_b, 0, h)

    def back_act(grad, p, scale, shift, pre_ref, slope_ref, right, row, h):
        grad_norm = dot_t(rows(grad, h, 0), p[...]) * slope_ref[h]
        right[h, pl.ds(shift, NB)] = (grad_norm * scale[...]).astype(BF16).reshape(NB, RB, F)
        nbs[row : row + 1] += jnp.sum(grad_norm * pre_ref[h], 0, keepdims=True)
        nbs[row + 1 : row + 2] += jnp.sum(grad_norm, 0, keepdims=True)

    def back_in(grad, w, shift, right, dst, h):
        total = rows(grad, h, 0).astype(F32)
        total = total + dot_t(rows(right, h, shift), w[1])
        total = total + dot_t(rows(right, h, 2 * shift), w[0])
        total = total + dot_t(rows(right, h, 0), w[2])
        dst[h] = total.astype(BF16).reshape(NB, RB, C)

    blocks = ((lt_a, rh_a, 2, own_a, giv_a), (lt_b, rh_b, 1, own_b, giv_b))

    def part(n, t, half, h):
        left, right, shift = blocks[n][:3]
        start = jnp.where(t == 3, ACT, 2 * shift - shift * t)
        value = dot(left[t // 3, h, pl.ds(half * 384, 384), :], rows(right, h, start))
        return value.reshape(4, 96, F)

    def core_copy(n, p):
        return remote(cs.at[n, p], cr.at[n, p], sem_cs.at[n, p], sem_cr.at[n, p], partner)

    def early_parts(n):
        own, giv = blocks[n][3:]

        def step(p):
            for half in range(2):
                giv[p, pl.ds(half * 4, 4)] = part(n, 2 * p + 1 - core, half, 0)
                own[p, pl.ds(half * 4, 4)] = part(n, 2 * p + core, half, 0)

        loop(2, step)

    def give_parts(n):
        giv = blocks[n][4]

        def step(p):
            for half in range(2):
                at = pl.ds(half * 4, 4)
                value = giv[p, at] + part(n, 2 * p + 1 - core, half, 1)
                cs[n, p, at] = value.astype(BF16)
            core_copy(n, p).start()

        loop(2, step)

    def keep_parts(n):
        own = blocks[n][3]

        def step(p):
            for half in range(2):
                at = pl.ds(half * 4, 4)
                own[p, at] += part(n, 2 * p + core, half, 1)

        loop(2, step)

    def exchange(src, dst, send, recv, mine, where, count):
        def copy(r):
            t = lax.rem(mine + 1 + r, count)
            return remote(src.at[t], dst.at[mine], send.at[t], recv.at[mine], where(t))

        def arrive(r):
            t = lax.rem(mine + 1 + r, count)
            pltpu.make_async_copy(dst.at[t], dst.at[t], recv.at[t]).wait()

        return (
            lambda: loop(count - 1, lambda r: copy(r).start()),
            lambda: loop(count - 1, arrive),
            lambda: loop(count - 1, lambda r: copy(r).wait_send()),
        )

    x1s, x1r, y1s, y1r = (x1s_a, x1s_b), (x1r_a, x1r_b), (y1s_a, y1s_b), (y1r_a, y1r_b)
    y2s, y2r, x2s, x2r = (y2s_a, y2s_b), (y2r_a, y2r_b), (x2s_a, x2s_b), (x2r_a, x2r_b)
    xs1 = [exchange(x1s[n], x1r[n], sx1.at[n], rx1.at[n], x, to_x, 4) for n in range(2)]
    ys1 = [exchange(y1s[n], y1r[n], sy1.at[n], ry1.at[n], y, to_y, 4) for n in range(2)]
    ys2 = [exchange(y2s[n], y2r[n], sy2.at[n], ry2.at[n], y, to_y, 4) for n in range(2)]
    xs2 = [exchange(x2s[n], x2r[n], sx2.at[n], rx2.at[n], x, to_x, 4) for n in range(2)]
    zs3 = exchange(zs, zr, sz, rz, z, to_z, 8)
    nb_core = remote(nbs, nbc, snc, rnc, partner)

    def join(n):
        own = blocks[n][3]

        def step(p):
            core_copy(n, p).wait_recv()
            for lo in range(2):
                for t in range(4):
                    total = (own[p, 4 * lo + t] + cr[n, p, 4 * lo + t].astype(F32)).astype(BF16)
                    x1s[n][2 * p + lo, 48 * t : 48 * t + 48] = total[0:48]
                    y1s[n][t, pl.ds(tile(96 * p + 48 * lo), 48)] = total[48:96]

        if n == 0:
            nb_core.wait_recv()
            for t in range(4):
                x1s[n][t, 192:208] = split(nbs[...] + nbc[...])
        loop(2, step)
        xs1[n][0]()
        ys1[n][0]()

    def total_of(src, recv, mine, at, size, count=4):
        total = src[mine, pl.ds(at, size)].astype(F32)
        for r in range(1, count):
            total = total + recv[lax.rem(mine + r, count), pl.ds(at, size)].astype(F32)
        return total

    def norms_of(src, recv, mine, at, count=4):
        total = total_of(src, recv, mine, at, 16, count)
        return total[0:8] + total[8:16]

    def second_step(n):
        xs1[n][1]()

        def lower(t):
            y2s[n][t, 0:48] = total_of(x1s[n], x1r[n], x, tile(48 * t), 48).astype(BF16)
            if n == 0:
                y2s[n][t, 48:64] = split(norms_of(x1s[n], x1r[n], x, 192))

        loop(4, lower)
        ys2[n][0]()
        ys1[n][1]()

        def upper(t):
            x2s[n][t] = total_of(y1s[n], y1r[n], y, tile(48 * t), 48).astype(BF16)

        loop(4, upper)
        xs2[n][0]()

    def third_step(n):
        ys2[n][1]()
        red[n, 0:48] = total_of(y2s[n], y2r[n], y, 0, 48)
        if n == 0:
            some = split(norms_of(y2s[n], y2r[n], y, 48))
            for t in range(8):
                zs[t, 32:48] = some
        xs2[n][1]()
        red[n, 48:96] = total_of(x2s[n], x2r[n], x, 0, 48)
        for t in range(8):
            zs[t, 16 * n : 16 * n + 16] = red[n, 12 * t : 12 * t + 16].astype(BF16)

    factor = 1.0 / math.sqrt(4 * NC * NB * 2 * RB)

    def spread(r):
        t = lax.rem(k + 1 + r, 4)
        return remote(fg.at[k], fg.at[k], sf.at[t], rf.at[k], to_k(t))

    def send_out(h):
        def step(n):
            for r in range(5):
                j, home, place = coming(n, r)
                src, dst, recv = gi.at[h, j], out.at[place, h], ro.at[h, place]

                @pl.when(home != d)
                def _():
                    remote(src, dst, so.at[h, j], recv, to_seq(home)).start()

                @pl.when(home == d)
                def _():
                    pltpu.make_async_copy(src, dst, recv).start()

        loop(4, step)

    def wait_c(h):
        loop(NB, lambda j: pltpu.make_async_copy(cot.at[0, h], c.at[h, j], rc.at[h, j]).wait())

    red[:, 96:104] = jnp.zeros((2, 8, F), F32)

    wait_c(0)
    back_act(c, pb, sb, 1, pr_b, sl_b, rh_b, 2, 0)
    turn(c, 0, lt_b, 1, 0)
    back_in(c, wb, 1, rh_b, gs, 0)
    back_act(gs, pa, sa, 2, pr_a, sl_a, rh_a, 0, 0)
    back_in(gs, wa, 2, rh_a, gi, 0)
    turn(gs, 0, lt_a, 1, 0)
    early_parts(1)
    early_parts(0)

    def sent_in(n):
        for r in range(5):
            i, target, _ = going(n, r)

            @pl.when(target != d)
            def _():
                remote(feat.at[i], u.at[:, 0], su.at[i], ru.at[0], to_seq(target)).wait_send()
                for h in range(2):
                    remote(
                        cot.at[i, h], c.at[h, 0], sc.at[h, i], rc.at[h, 0], to_seq(target)
                    ).wait_send()

    def sent_out(n):
        for r in range(5):
            j, home, _ = coming(n, r)

            @pl.when(home != d)
            def _():
                for h in range(2):
                    remote(
                        gi.at[h, j], out.at[0, h], so.at[h, j], ro.at[h, 0], to_seq(home)
                    ).wait_send()

    wait_c(1)
    send_out(0)
    back_act(c, pb, sb, 1, pr_b, sl_b, rh_b, 2, 1)
    turn(c, 0, lt_b, 1, 1)
    give_parts(1)
    keep_parts(1)
    back_in(c, wb, 1, rh_b, gs, 1)
    join(1)
    back_act(gs, pa, sa, 2, pr_a, sl_a, rh_a, 0, 1)
    nb_core.start()
    turn(gs, 0, lt_a, 1, 1)
    give_parts(0)
    keep_parts(0)
    join(0)
    back_in(gs, wa, 2, rh_a, gi, 1)
    send_out(1)
    loop(4, sent_in)
    second_step(1)
    nb_core.wait_send()
    for n in range(2):
        for p in range(2):
            core_copy(n, p).wait_send()
    second_step(0)
    third_step(1)
    for step in (xs1, ys1):
        for n in range(2):
            step[n][2]()
    third_step(0)
    zs3[0]()
    for step in (xs2, ys2):
        for n in range(2):
            step[n][2]()
    zs3[1]()
    fg[k] = total_of(zs, zr, z, 0, 32, 8) * factor
    loop(3, lambda r: spread(r).start())
    norms[...] = norms_of(zs, zr, z, 32, 8) * factor
    zs3[2]()
    loop(4, sent_out)
    for h in range(2):
        loop(NB, lambda i: pltpu.make_async_copy(cot.at[0, h], out.at[i, h], ro.at[h, i]).wait())
    for r in range(3):
        t = lax.rem(k + 1 + r, 4)
        pltpu.make_async_copy(fg.at[t], fg.at[t], rf.at[t]).wait()
        spread(r).wait_send()
    fin[...] = fg[...]


def finish(grad, fin, norms, out, gca, gpa, gsa, gba, gcb, gpb, gsb, gbb, held, fv, nv, v0, v1, v2, v3, q0, q1, p0, p1, ins, outs):
    def copy(src, dst, sem):
        return pltpu.make_async_copy(src, dst, sem)

    parts = 4
    each = grad.shape[0] // parts
    at = [pl.ds(n * each, each) for n in range(parts)]
    into = [copy(norms, nv, ins.at[0]), copy(fin, fv, ins.at[1])]
    into += [copy(grad.at[at[n]], held.at[at[n]], ins.at[2 + n]) for n in range(parts)]
    onto = [copy(v, o, outs.at[n]) for n, (v, o) in enumerate(zip((v0, v1, v2, v3), (gsa, gba, gsb, gbb)))]
    onto += [copy(v, o, outs.at[4 + n]) for n, (v, o) in enumerate(zip((q0, q1, p0, p1), (gca, gcb, gpa, gpb)))]
    onto += [copy(held.at[at[n]], out.at[at[n]], outs.at[8 + n]) for n in range(parts)]
    for one in into:
        one.start()
    into[0].wait()
    for n, v in enumerate((v0, v1, v2, v3)):
        v[...] = nv[n]
        onto[n].start()
    into[1].wait()
    for n, (conv, point) in enumerate(((q0, p0), (q1, p1))):
        for t in range(3):
            conv[t] = fv[t, 16 * n : 16 * n + 12]
        point[...] = fv[3, 16 * n : 16 * n + 12]
    for n in range(4, 8):
        onto[n].start()
    for n in range(parts):
        into[2 + n].wait()
        onto[8 + n].start()
    for one in onto:
        one.wait()


def body(feat, wa, sa, ba, pa, wb, sb, bb, pb, cot):
    feat = feat.reshape(NB, 2, RB, C)
    cot = cot.reshape(NB, 2, RB, C)
    hbm = pl.BlockSpec(memory_space=pltpu.HBM)
    vmem = pl.BlockSpec(memory_space=pltpu.VMEM)
    dma = pltpu.SemaphoreType.DMA

    def bins(count, width=C):
        return pltpu.VMEM((2, count, RB, width), BF16)

    def terms(*dims):
        return pltpu.VMEM(dims + (F,), BF16)

    flat = pltpu.VMEM((2, HALF, F), F32)
    whole = pltpu.VMEM((2, 8, 96, F), F32)
    turned = pltpu.VMEM((2, 2, C, HALF), BF16)
    scratch = (
        [bins(NB + 4), bins(NB), bins(NB + 2), bins(NB), bins(NB)]
        + [flat] * 4
        + [bins(ACT + NB, F)] * 2
        + [turned] * 2
        + [pltpu.VMEM((3, C, F), BF16)] * 2
        + [pltpu.VMEM((F, C), BF16)] * 2
        + [pltpu.VMEM((F,), F32)] * 4
        + [whole] * 4
        + [terms(2, 2, 8, 96)] * 2
        + [terms(4, 208)] * 2
        + [terms(4, 192)] * 6
        + [terms(4, 64)] * 2
        + [terms(4, 48)] * 6
        + [pltpu.VMEM((2, 104, F), F32)]
        + [terms(8, 48)] * 2
        + [pltpu.VMEM((4, 32, F), F32)]
        + [pltpu.VMEM((8, F), F32)] * 2
        + [dma((8,)), dma((NB,)), dma((NB,))]
        + [dma((2, NB))] * 4
        + [dma((2, 2))] * 2
        + [dma((2, 4))] * 8
        + [dma((8,))] * 2
        + [dma((4,))] * 2
        + [dma] * 2
    )
    shape = jax.ShapeDtypeStruct
    grad, fin, norms = pl.pallas_call(
        kernel,
        out_shape=[shape((NB, 2, RB, C), BF16), shape((4, 32, F), F32), shape((8, F), F32)],
        in_specs=[hbm] * 10,
        out_specs=[hbm, vmem, vmem],
        scratch_shapes=scratch,
        compiler_params=pltpu.CompilerParams(
            collective_id=0, has_side_effects=True, vmem_limit_bytes=58 << 20
        ),
        cost_estimate=pl.CostEstimate(
            flops=23 * 2 * 640 * C * F, bytes_accessed=8 << 20, transcendentals=1 << 20
        ),
        name="blocks",
    )(feat, wa, sa, ba, pa, wb, sb, bb, pb, cot)
    small = [shape((3, 12, F), F32), shape((12, F), F32), shape((F,), F32), shape((F,), F32)]
    grad, gca, gpa, gsa, gba, gcb, gpb, gsb, gbb = pl.pallas_call(
        finish,
        out_shape=[shape((NB * 2 * RB, C), BF16)] + small * 2,
        in_specs=[hbm] * 3,
        out_specs=[hbm] * 9,
        scratch_shapes=[
            pltpu.VMEM((NB * 2 * RB, C), BF16), pltpu.VMEM((4, 32, F), F32), pltpu.VMEM((8, F), F32),
            *[pltpu.VMEM((F,), F32)] * 4, *[pltpu.VMEM((3, 12, F), F32)] * 2,
            *[pltpu.VMEM((12, F), F32)] * 2, dma((6,)), dma((12,)),
        ],
        name="finish",
    )(grad.reshape(NB * 2 * RB, C), fin, norms)
    return (grad[None], gca, gpa.T, gsa, gba, gcb, gpb.T, gsb, gbb)


def solution(mesh):
    bins = P("chrom", "seq", None)
    taps, projection = P(None, "seq", None), P(None, "seq")
    in_specs = (bins,) + (P(),) * 8 + (bins,)
    out_specs = (bins,) + (taps, projection, P(), P()) * 2
    return jax.shard_map(body, mesh=mesh, in_specs=in_specs, out_specs=out_specs, check_vma=False)
```
